32 devices in a mesh: groups: 2 (over y), replica: 8 (over z, x), tensor: 2 (over core).
Axes of the slice: x: 2, y: 2, z: 4, core: 2. Of those that a mesh axis runs over, the one named last changes fastest.
Arguments:
- hidden: bfloat16 [192, 8192], P(('groups', 'replica'), 'tensor'), parts along dimension 0, may hold values from -6 to 6
- rollout_lengths: int32 [64], P('groups'), parts along dimension 0, may hold values from 1 to 3
- source_replica: int32 [64], P('groups'), parts along dimension 0, may hold values from 0 to 7, as said below
- page_table: int32 [64, 3], P('groups'), parts along dimension 0, may hold values from 0 to 191, as said below
- x_new: bfloat16 [2, 64, 8192], P(None, 'groups', 'tensor'), parts along dimension 1, may hold values from -6 to 6
- norm_attn: float32 [8192], P('tensor'), may hold values from 0.5 to 1.5
- norm_ffn: float32 [8192], P('tensor'), may hold values from 0.5 to 1.5
- w_query: bfloat16 [8192, 8192], P('tensor', 'replica'), may hold values from -0.0625 to 0.0625
- w_keyval: bfloat16 [8192, 2, 8192], P('tensor', None, 'replica'), may hold values from -0.0625 to 0.0625
- qkv_bias: float32 [3, 8192], P(None, 'replica'), may hold values from -7 to 7
- w_out: bfloat16 [8192, 8192], P('replica', 'tensor'), may hold values from -0.0625 to 0.0625
- w_gateup: bfloat16 [8192, 2, 12288], P('tensor', None, 'replica'), may hold values from -0.0625 to 0.0625
- w_down: bfloat16 [12288, 8192], P('replica', 'tensor'), may hold values from -0.0546875 to 0.0546875
Outputs:
- decoded: bfloat16 [2, 64, 8192], P(None, 'groups', 'tensor'), parts along dimension 1
- kv_pool: bfloat16 [2, 384, 8192], P(None, ('groups', 'tensor'), 'replica'), parts along dimension 1
The draws below stay inside these ranges and needn't reach their ends.
There are 2 independent parts, one for each index of `groups`. The reference program is written for one: setup_inputs(seed, part) draws one part's arguments, and reference() takes and returns one part's arrays. A program takes and returns all parts, laid end to end along the dimension named above; an argument that names none is the same for every part. Nothing has to cross between parts.
Inputs may be any that keep to these rules, and one draw needn't show every extreme that they name: `source_replica`: rollouts on one source replica have together at most 12 cached rows, and in every draw some source replica holds exactly 12; at most 4 rollouts share a source. `page_table`: all entries are distinct.
All inputs are finite; a program needn't handle non-finite values.
Results may differ from the reference program's by a relative error of at most 0.0169.
Values may be sent and summed in bfloat16 or wider, within the bound.
A program may use at most 256 MiB of HBM per device.

```python
import jax
import jax.numpy as jnp
from jax import lax

D = 8192
HEADS = 64
HD = 128
FF = 12288
ROLL = 32
STEPS = 2
SLOTS = 12
MAXLEN = 3
POOL = 192
N_REPLICA = 8


def rollout_layout(key):
    key_src, key_len, key_pick = jax.random.split(key, 3)
    shuffled = jax.random.permutation(key_src, N_REPLICA)
    sources = shuffled[jnp.arange(ROLL) % N_REPLICA]
    lowest = max(1, MAXLEN // 2)
    lengths = jax.random.randint(key_len, (ROLL,), lowest, MAXLEN + 1)
    chosen = jax.random.randint(key_pick, (), 0, ROLL)
    lengths = jnp.where(sources == sources[chosen], MAXLEN, lengths)
    return (lengths.astype(jnp.int32), sources.astype(jnp.int32))


def draw_rollout_lengths(key, part):
    return rollout_layout(key)[0]


def draw_source_replica(key, part):
    return rollout_layout(key)[1]


def draw_page_table(key, part):
    key = jax.random.fold_in(key, 7)
    shuffled = jax.random.permutation(key, POOL)
    return shuffled[:ROLL * MAXLEN].reshape(ROLL, MAXLEN).astype(jnp.int32)


def draw_qkv_bias(key, part):
    key = jax.random.fold_in(key, 11)
    key_amp, key_top, key_low, key_sign, key_one, key_two, key_val = jax.random.split(key, 7)
    head_ids = jnp.arange(HEADS)
    amplitude = jnp.exp(jax.random.uniform(key_amp, (HEADS,), jnp.float32, jnp.log(0.5), jnp.log(5.5)))
    top_head = jax.random.randint(key_top, (), 0, HEADS)
    low_head = (top_head + 1 + jax.random.randint(key_low, (), 0, max(1, HEADS - 1))) % HEADS
    amplitude = jnp.where(head_ids == top_head, 5.5, amplitude)
    amplitude = jnp.where((head_ids == low_head) & (head_ids != top_head), 0.5, amplitude)
    spread = jnp.repeat(amplitude, HD)
    signs = jnp.where(jax.random.bernoulli(key_sign, 0.5, (HEADS * HD,)), 1.0, -1.0)
    first = jax.random.uniform(key_one, (HEADS * HD,), jnp.float32, 0.8, 1.2)
    second = jax.random.uniform(key_two, (HEADS * HD,), jnp.float32, 0.8, 1.2)
    query_bias = spread * signs * first
    key_bias = spread * signs * second
    value_bias = jnp.clip(0.5 * jax.random.normal(key_val, (HEADS * HD,), jnp.float32), -3.0, 3.0)
    return jnp.stack([query_bias, key_bias, value_bias]).astype(jnp.float32)


def shard_levels(key, dims, pieces, least, high):
    factor_of = 1.0
    for dim, shards_of in pieces:
        draws = jax.random.uniform(jax.random.fold_in(jax.random.fold_in(key, 6), dim), (shards_of,), jnp.float32, least / len(pieces), high / len(pieces))
        factor_of = factor_of * jnp.repeat(jnp.exp(draws), dims[dim] // shards_of).reshape((-1,) + (1,) * (len(dims) - 1 - dim))
    return factor_of


def bell_draw(stream_key, dims, deviation, bound, shards=(), held_as=jnp.bfloat16):
    gain = shard_levels(stream_key, dims, shards, -0.22, 0.18) if shards else 1.0
    values = jax.random.normal(stream_key, dims, jnp.float32) * deviation * gain
    return jnp.minimum(jnp.maximum(values, -bound), bound).astype(held_as)


def setup_inputs(seed: int = 0, part: int = 0) -> dict:
    key_of = jax.random.split(jax.random.key(seed), 14)
    part_splits = jax.random.split(jax.random.fold_in(key_of[13], part), 14)
    hidden = bell_draw(part_splits[0], (N_REPLICA * SLOTS, D), 1.0, 6.0, ((0, 8), (1, 2)))
    rollout_lengths = draw_rollout_lengths(jax.random.fold_in(jax.random.fold_in(key_of[13], part), 71), part)
    source_replica = draw_source_replica(jax.random.fold_in(jax.random.fold_in(key_of[13], part), 71), part)
    page_table = draw_page_table(jax.random.fold_in(jax.random.fold_in(key_of[13], part), 71), part)
    x_new = bell_draw(part_splits[4], (STEPS, ROLL, D), 1.0, 6.0, ((2, 2),))
    norm_attn = jnp.clip(1.0 + 0.1 * jax.random.normal(key_of[5], (D,), jnp.float32), 0.5, 1.5)
    norm_ffn = jnp.clip(1.0 + 0.1 * jax.random.normal(key_of[6], (D,), jnp.float32), 0.5, 1.5)
    w_query = bell_draw(key_of[7], (D, HEADS * HD), D ** -0.5, 0.0625, ((0, 2), (1, 8)))
    w_keyval = bell_draw(key_of[8], (D, 2, HEADS * HD), D ** -0.5, 0.0625, ((0, 2), (2, 8)))
    qkv_bias = draw_qkv_bias(jax.random.fold_in(key_of[13], 71), part)
    w_out = bell_draw(key_of[10], (HEADS * HD, D), (HEADS * HD) ** -0.5, 0.0625, ((0, 8), (1, 2)))
    w_gateup = bell_draw(key_of[11], (D, 2, FF), D ** -0.5, 0.0625, ((0, 2), (2, 8)))
    w_down = bell_draw(key_of[12], (FF, D), FF ** -0.5, 0.0546875, ((0, 8), (1, 2)))
    return {"hidden": hidden, "rollout_lengths": rollout_lengths, "source_replica": source_replica, "page_table": page_table, "x_new": x_new, "norm_attn": norm_attn, "norm_ffn": norm_ffn, "w_query": w_query, "w_keyval": w_keyval, "qkv_bias": qkv_bias, "w_out": w_out, "w_gateup": w_gateup, "w_down": w_down}


EPSILON = 1e-06
NEGATIVE = -1e+30

def project(token_rows, gain_vec, weight):
    wide = token_rows.astype(jnp.float32)
    row_scale = lax.rsqrt(lax.optimization_barrier(jnp.mean(wide * wide, axis=1, keepdims=True)) + EPSILON)
    scaled = (wide * gain_vec).astype(jnp.bfloat16)
    return row_scale * jnp.dot(scaled, weight, preferred_element_type=jnp.float32)

def reference(hidden, rollout_lengths, source_replica, page_table, x_new, norm_attn, norm_ffn, w_query, w_keyval, qkv_bias, w_out, w_gateup, w_down):
    head_cols = HEADS * HD
    sequence = jnp.arange(ROLL, dtype=jnp.int32)
    earlier = (source_replica[:, None] == source_replica[None, :]) & (sequence[None, :] < sequence[:, None])
    offsets = lax.optimization_barrier(jnp.sum(jnp.where(earlier, rollout_lengths[None, :], 0), axis=1)).astype(jnp.int32)
    places = jnp.arange(MAXLEN, dtype=jnp.int32)
    is_valid = places[None, :] < rollout_lengths[:, None]
    slot_index = jnp.clip(source_replica[:, None] * SLOTS + offsets[:, None] + places[None, :], 0, N_REPLICA * SLOTS - 1).astype(jnp.int32)
    token_rows = hidden[slot_index.reshape(-1)]
    keyval_flat = w_keyval.reshape(D, 2 * head_cols)
    key_vals = project(token_rows, norm_attn, keyval_flat) + qkv_bias[1:].reshape(1, 2 * head_cols)
    key_vals = key_vals.astype(jnp.bfloat16).reshape(ROLL, MAXLEN, 2, head_cols)
    targets = jnp.where(is_valid, page_table, POOL).astype(jnp.int32)
    stacked = jnp.transpose(key_vals.reshape(ROLL * MAXLEN, 2, head_cols), (1, 0, 2))
    kv_pool = jnp.zeros((2, POOL, head_cols), jnp.bfloat16).at[:, targets.reshape(-1)].set(stacked, mode='drop')
    cache_keys = key_vals[:, :, 0]
    cache_vals = key_vals[:, :, 1]
    weight_all = jnp.concatenate([w_query, keyval_flat], axis=1)
    new_keys = []
    new_vals = []
    decoded_rows = []
    for turn_index in range(STEPS):
        x_rows = x_new[turn_index]
        qkv_rows = project(x_rows, norm_attn, weight_all) + qkv_bias.reshape(1, 3 * head_cols)
        query = qkv_rows[:, :head_cols].astype(jnp.bfloat16)
        new_keys.append(qkv_rows[:, head_cols:2 * head_cols].astype(jnp.bfloat16))
        new_vals.append(qkv_rows[:, 2 * head_cols:].astype(jnp.bfloat16))
        key_rows = jnp.concatenate([cache_keys] + [item[:, None] for item in new_keys], axis=1)
        val_rows = jnp.concatenate([cache_vals] + [item[:, None] for item in new_vals], axis=1)
        live_mask = jnp.concatenate([is_valid, jnp.ones((ROLL, turn_index + 1), bool)], axis=1)
        length_all = key_rows.shape[1]
        query_wide = query.astype(jnp.float32).reshape(ROLL, HEADS, HD)
        key_wide = key_rows.astype(jnp.float32).reshape(ROLL, length_all, HEADS, HD)
        val_wide = val_rows.astype(jnp.float32).reshape(ROLL, length_all, HEADS, HD)
        scores = jnp.einsum('rhd,rlhd->rhl', query_wide, key_wide) / jnp.sqrt(jnp.float32(HD))
        scores = jnp.where(live_mask[:, None, :], scores, NEGATIVE)
        peak_val = lax.optimization_barrier(jnp.max(scores, axis=-1, keepdims=True))
        weights = jnp.exp(scores - peak_val)
        totals = lax.optimization_barrier(jnp.sum(weights, axis=-1))
        rounded = weights.astype(jnp.bfloat16).astype(jnp.float32)
        accum = jnp.einsum('rhl,rlhd->rhd', rounded, val_wide)
        attended = (accum / totals[:, :, None]).reshape(ROLL, head_cols).astype(jnp.bfloat16)
        middle = x_rows.astype(jnp.float32) + jnp.dot(attended, w_out, preferred_element_type=jnp.float32)
        gate_up = project(middle, norm_ffn, w_gateup.reshape(D, 2 * FF))
        hidden_mid = (jax.nn.silu(gate_up[:, :FF]) * gate_up[:, FF:]).astype(jnp.bfloat16)
        result = middle + jnp.dot(hidden_mid, w_down, preferred_element_type=jnp.float32)
        decoded_rows.append(result.astype(jnp.bfloat16))
    return (jnp.stack(decoded_rows), kv_pool)
```

```python
import jax
import jax.numpy as jnp
from jax import lax
from jax.sharding import PartitionSpec as P

D = 8192
HD = 128
STEPS = 2


EPSILON = 1e-06
NEGATIVE = -1e30


def partner(array, axis, bit):
    return lax.ppermute(array, axis, [(i, i ^ 1 << bit) for i in range(lax.axis_size(axis))])


def merged(part, axis, combine):
    gathered = jax.tree.map(lambda a: lax.all_gather(a, axis), part)

    def take(source):
        return jax.tree.map(lambda a: lax.dynamic_index_in_dim(a, source, 0, False), gathered)

    return lax.fori_loop(
        1, lax.axis_size(axis), lambda source, state: combine(state, take(source)), take(0)
    )


def per_device(
    hidden,
    rollout_lengths,
    source_replica,
    page_table,
    x_new,
    norm_attn,
    norm_ffn,
    w_query,
    w_keyval,
    qkv_bias,
    w_out,
    w_gateup,
    w_down,
):
    replicas = lax.axis_size("replica")
    slots = hidden.shape[0]
    half_width = hidden.shape[1]
    columns = w_query.shape[1]
    rollouts = rollout_lengths.shape[0]
    longest = page_table.shape[1]
    pool_rows = 2 * rollouts * longest
    half_rows = pool_rows // 2
    units = w_down.shape[0]
    keyval_flat = w_keyval.reshape(half_width, 2 * columns)
    sequence = jnp.arange(rollouts, dtype=jnp.int32)
    earlier = (source_replica[:, None] == source_replica[None, :]) & (
        sequence[None, :] < sequence[:, None]
    )
    offsets = jnp.sum(jnp.where(earlier, rollout_lengths[None, :], 0), axis=1)
    places = jnp.arange(longest, dtype=jnp.int32)
    is_valid = places[None, :] < rollout_lengths[:, None]
    targets = jnp.where(is_valid, page_table, pool_rows)
    owners = (
        jnp.full((pool_rows,), -1, jnp.int32)
        .at[targets.reshape(-1)]
        .set(jnp.broadcast_to(sequence[:, None], (rollouts, longest)).reshape(-1), mode="drop")
    )
    empty = (jnp.zeros((pool_rows, 2 * columns), jnp.float32), jnp.zeros((pool_rows,), jnp.float32))
    slot_index = source_replica[:, None] * slots + offsets[:, None] + places[None, :]
    slot_index = jnp.where(is_valid, slot_index, replicas * slots)
    lookup = (
        jnp.full((replicas * slots,), pool_rows, jnp.int32)
        .at[slot_index.reshape(-1)]
        .set(targets.reshape(-1), mode="drop")
    )
    block_rows = lax.all_gather(hidden, "replica", axis=0, tiled=True)
    wide = block_rows.astype(jnp.float32)
    make_scaled = (wide * norm_attn).astype(jnp.bfloat16)
    partial_kv = jnp.dot(make_scaled, keyval_flat, preferred_element_type=jnp.float32)
    make_squares = jnp.sum(wide * wide, axis=1)
    part_pool = empty[0].at[lookup].add(partial_kv, mode="drop")
    stat_pool = empty[1].at[lookup].add(make_squares, mode="drop")
    part_half, stat_half = (
        lax.psum_scatter(
            part_pool.astype(jnp.bfloat16), "tensor", scatter_dimension=0, tiled=True
        ).astype(jnp.float32),
        lax.psum_scatter(
            stat_pool.astype(jnp.bfloat16), "tensor", scatter_dimension=0, tiled=True
        ).astype(jnp.float32),
    )
    tensor_index = lax.axis_index("tensor")
    owner_half = lax.dynamic_slice_in_dim(owners, tensor_index * half_rows, half_rows)
    filled = (owner_half >= 0)[:, None]
    row_scale = lax.rsqrt(stat_half / D + EPSILON)[:, None]
    kv_half = jnp.where(
        filled, row_scale * part_half + qkv_bias[1:].reshape(1, 2 * columns), 0.0
    ).astype(jnp.bfloat16)
    kv_out = jnp.transpose(kv_half.reshape(half_rows, 2, columns), (1, 0, 2))
    cache_keys = kv_half[:, :columns].astype(jnp.float32)
    cache_vals = kv_half[:, columns:].astype(jnp.float32)
    heads_here = max(1, columns // HD)
    piece_width = columns // heads_here
    group_size = HD // piece_width
    bit_count = group_size.bit_length() - 1
    inverse = 1.0 / jnp.sqrt(jnp.float32(HD))
    onehot = owner_half[:, None] == sequence[None, :]
    onehot_half = onehot.astype(jnp.bfloat16)
    onehot_wide = onehot.astype(jnp.float32)
    keep_new = tensor_index == 0

    def spread_out(values):
        return jnp.repeat(values, piece_width, axis=-1)

    def combine(first, second):
        peak_val = jnp.maximum(first[0], second[0])
        scale_one = jnp.exp(first[0] - peak_val)
        scale_two = jnp.exp(second[0] - peak_val)
        return (
            peak_val,
            first[1] * scale_one + second[1] * scale_two,
            first[2] * spread_out(scale_one) + second[2] * spread_out(scale_two),
        )

    new_count = STEPS * rollouts
    x_wide = x_new.reshape(new_count, half_width).astype(jnp.float32)
    scaled = (x_wide * norm_attn).astype(jnp.bfloat16)
    query_part = jnp.dot(scaled, w_query, preferred_element_type=jnp.float32)
    keyval_part = jnp.dot(scaled, keyval_flat, preferred_element_type=jnp.float32)
    squares = jnp.sum(x_wide * x_wide, axis=1, keepdims=True)
    fused = jnp.concatenate(
        [query_part, keyval_part, jnp.broadcast_to(squares, (new_count, 128))], axis=1
    )
    fused = lax.psum(fused, "tensor")
    step_scale = lax.rsqrt(fused[:, 3 * columns : 3 * columns + 1] / D + EPSILON)
    rows_new = (step_scale * fused[:, : 3 * columns] + qkv_bias.reshape(1, 3 * columns)).astype(
        jnp.bfloat16
    )
    rows_new = rows_new.reshape(STEPS, rollouts, 3 * columns)
    queries = rows_new[:, :, :columns]
    new_keys = rows_new[:, :, columns : 2 * columns]
    new_vals = rows_new[:, :, 2 * columns :]
    pooled_query = jnp.stack(
        [
            jnp.dot(onehot_half, queries[s], preferred_element_type=jnp.float32)
            for s in range(STEPS)
        ]
    )
    cache_all = jnp.sum(
        (pooled_query * cache_keys[None]).reshape(STEPS, half_rows, heads_here, piece_width),
        axis=-1,
    )
    new_all = jnp.sum(
        (
            queries.astype(jnp.float32)[:, None] * new_keys.astype(jnp.float32)[None]
        ).reshape(STEPS, STEPS, rollouts, heads_here, piece_width),
        axis=-1,
    )
    for bit_index in range(bit_count):
        swapped = partner((cache_all, new_all), "replica", bit_index)
        cache_all = cache_all + swapped[0]
        new_all = new_all + swapped[1]
    parts = []
    for turn_index in range(STEPS):
        cache_scores = jnp.where(filled, cache_all[turn_index] * inverse, NEGATIVE)
        new_scores = jnp.where(
            keep_new, new_all[turn_index, : turn_index + 1] * inverse, NEGATIVE
        )
        segment_top = jnp.max(
            jnp.where(onehot[:, :, None], cache_scores[:, None, :], NEGATIVE), axis=0
        )
        peak_val = jnp.maximum(segment_top, jnp.max(new_scores, axis=0))
        row_peak = jnp.dot(onehot_wide, peak_val, precision=lax.Precision.HIGHEST)
        cache_weights = jnp.exp(cache_scores - row_peak)
        new_weights = jnp.where(keep_new, jnp.exp(new_scores - peak_val[None]), 0.0)
        totals = jnp.dot(onehot_wide.T, cache_weights, precision=lax.Precision.HIGHEST) + jnp.sum(
            new_weights, axis=0
        )
        cache_rounded = spread_out(cache_weights.astype(jnp.bfloat16).astype(jnp.float32))
        accum = jnp.dot(onehot_wide.T, cache_rounded * cache_vals, precision=lax.Precision.HIGHEST)
        for item_index in range(turn_index + 1):
            new_rounded = spread_out(
                new_weights[item_index].astype(jnp.bfloat16).astype(jnp.float32)
            )
            accum = accum + new_rounded * new_vals[item_index].astype(jnp.float32)
        parts.append(jnp.concatenate([accum, totals, peak_val], axis=1))
    mine = jnp.stack(parts).reshape(new_count, columns + 2 * heads_here)
    both = lax.all_gather(mine, "tensor")

    def split(block):
        return block[:, columns + heads_here :], block[:, columns : columns + heads_here], block[:, :columns]

    _, total_all, accum_all = combine(split(both[0]), split(both[1]))
    attended = (accum_all / spread_out(total_all)).astype(jnp.bfloat16)
    attn_part = jnp.dot(attended, w_out, preferred_element_type=jnp.float32)
    middle = x_wide + lax.psum(attn_part, "replica")
    scaled_mid = (middle * norm_ffn).astype(jnp.bfloat16)
    gate_up = jnp.dot(
        scaled_mid, w_gateup.reshape(half_width, 2 * units), preferred_element_type=jnp.float32
    )
    mid_squares = jnp.sum(middle * middle, axis=1, keepdims=True)
    fused_mid = lax.psum(
        jnp.concatenate([gate_up, jnp.broadcast_to(mid_squares, (new_count, 128))], axis=1),
        "tensor",
    )
    mid_scale = lax.rsqrt(fused_mid[:, 2 * units : 2 * units + 1] / D + EPSILON)
    gate_vals = mid_scale * fused_mid[:, :units]
    up_vals = mid_scale * fused_mid[:, units : 2 * units]
    hidden_mid = (jax.nn.silu(gate_vals) * up_vals).astype(jnp.bfloat16)
    down_part = jnp.dot(hidden_mid, w_down, preferred_element_type=jnp.float32)
    result = middle + lax.psum(down_part, "replica")
    decoded = result.astype(jnp.bfloat16).reshape(STEPS, rollouts, half_width)
    return (decoded, kv_out)


def solution(mesh):
    placed = (
        P(("groups", "replica"), "tensor"),
        P("groups"),
        P("groups"),
        P("groups", None),
        P(None, "groups", "tensor"),
        P("tensor"),
        P("tensor"),
        P("tensor", "replica"),
        P("tensor", None, "replica"),
        P(None, "replica"),
        P("replica", "tensor"),
        P("tensor", None, "replica"),
        P("replica", "tensor"),
    )
    return jax.shard_map(
        per_device,
        mesh=mesh,
        in_specs=placed,
        out_specs=(P(None, "groups", "tensor"), P(None, ("groups", "tensor"), "replica")),
        check_vma=False,
    )
```

```python
import jax
import jax.numpy as jnp
from jax import lax
from jax.experimental import pallas as pl
from jax.experimental.pallas import tpu as pltpu
from jax.sharding import PartitionSpec as P

D = 8192
HD = 128
STEPS = 2


EPSILON = 1e-06
NEGATIVE = -1e30


def partner(array, axis, bit):
    return lax.ppermute(array, axis, [(i, i ^ 1 << bit) for i in range(lax.axis_size(axis))])


def merged(part, axis, combine):
    gathered = jax.tree.map(lambda a: lax.all_gather(a, axis), part)

    def take(source):
        return jax.tree.map(lambda a: lax.dynamic_index_in_dim(a, source, 0, False), gathered)

    return lax.fori_loop(
        1, lax.axis_size(axis), lambda source, state: combine(state, take(source)), take(0)
    )


def per_device(
    hidden,
    rollout_lengths,
    source_replica,
    page_table,
    x_new,
    norm_attn,
    norm_ffn,
    w_query,
    w_keyval,
    qkv_bias,
    w_out,
    w_gateup,
    w_down,
):
    replicas = lax.axis_size("replica")
    slots = hidden.shape[0]
    half_width = hidden.shape[1]
    columns = w_query.shape[1]
    rollouts = rollout_lengths.shape[0]
    longest = page_table.shape[1]
    pool_rows = 2 * rollouts * longest
    half_rows = pool_rows // 2
    units = w_down.shape[0]
    keyval_flat = w_keyval.reshape(half_width, 2 * columns)
    sequence = jnp.arange(rollouts, dtype=jnp.int32)
    earlier = (source_replica[:, None] == source_replica[None, :]) & (
        sequence[None, :] < sequence[:, None]
    )
    offsets = jnp.sum(jnp.where(earlier, rollout_lengths[None, :], 0), axis=1)
    places = jnp.arange(longest, dtype=jnp.int32)
    is_valid = places[None, :] < rollout_lengths[:, None]
    targets = jnp.where(is_valid, page_table, pool_rows)
    owners = (
        jnp.full((pool_rows,), -1, jnp.int32)
        .at[targets.reshape(-1)]
        .set(jnp.broadcast_to(sequence[:, None], (rollouts, longest)).reshape(-1), mode="drop")
    )
    empty = (jnp.zeros((pool_rows, 2 * columns), jnp.float32), jnp.zeros((pool_rows,), jnp.float32))
    slot_index = source_replica[:, None] * slots + offsets[:, None] + places[None, :]
    slot_index = jnp.where(is_valid, slot_index, replicas * slots)
    lookup = (
        jnp.full((replicas * slots,), pool_rows, jnp.int32)
        .at[slot_index.reshape(-1)]
        .set(targets.reshape(-1), mode="drop")
    )
    block_rows = lax.all_gather(hidden, "replica", axis=0, tiled=True)
    wide = block_rows.astype(jnp.float32)
    make_scaled = (wide * norm_attn).astype(jnp.bfloat16)
    partial_kv = jnp.dot(make_scaled, keyval_flat, preferred_element_type=jnp.float32)
    make_squares = jnp.sum(wide * wide, axis=1)
    part_pool = empty[0].at[lookup].add(partial_kv, mode="drop")
    stat_pool = empty[1].at[lookup].add(make_squares, mode="drop")
    part_half, stat_half = (
        lax.psum_scatter(
            part_pool.astype(jnp.bfloat16), "tensor", scatter_dimension=0, tiled=True
        ).astype(jnp.float32),
        lax.psum_scatter(
            stat_pool.astype(jnp.bfloat16), "tensor", scatter_dimension=0, tiled=True
        ).astype(jnp.float32),
    )
    tensor_index = lax.axis_index("tensor")
    owner_half = lax.dynamic_slice_in_dim(owners, tensor_index * half_rows, half_rows)
    filled = (owner_half >= 0)[:, None]
    row_scale = lax.rsqrt(stat_half / D + EPSILON)[:, None]
    kv_half = jnp.where(
        filled, row_scale * part_half + qkv_bias[1:].reshape(1, 2 * columns), 0.0
    ).astype(jnp.bfloat16)
    kv_out = jnp.transpose(kv_half.reshape(half_rows, 2, columns), (1, 0, 2))
    cache_keys = kv_half[:, :columns].astype(jnp.float32)
    cache_vals = kv_half[:, columns:].astype(jnp.float32)
    heads_here = max(1, columns // HD)
    piece_width = columns // heads_here
    group_size = HD // piece_width
    bit_count = group_size.bit_length() - 1
    inverse = 1.0 / jnp.sqrt(jnp.float32(HD))
    onehot = owner_half[:, None] == sequence[None, :]
    onehot_half = onehot.astype(jnp.bfloat16)
    onehot_wide = onehot.astype(jnp.float32)
    keep_new = tensor_index == 0

    def spread_out(values):
        return jnp.repeat(values, piece_width, axis=-1)

    def combine(first, second):
        peak_val = jnp.maximum(first[0], second[0])
        scale_one = jnp.exp(first[0] - peak_val)
        scale_two = jnp.exp(second[0] - peak_val)
        return (
            peak_val,
            first[1] * scale_one + second[1] * scale_two,
            first[2] * spread_out(scale_one) + second[2] * spread_out(scale_two),
        )

    new_count = STEPS * rollouts
    x_wide = x_new.reshape(new_count, half_width).astype(jnp.float32)
    scaled = (x_wide * norm_attn).astype(jnp.bfloat16)
    query_part = jnp.dot(scaled, w_query, preferred_element_type=jnp.float32)
    keyval_part = jnp.dot(scaled, keyval_flat, preferred_element_type=jnp.float32)
    squares = jnp.sum(x_wide * x_wide, axis=1, keepdims=True)
    fused = jnp.concatenate(
        [query_part, keyval_part, jnp.broadcast_to(squares, (new_count, 128))], axis=1
    )
    fused = lax.psum(fused, "tensor")
    step_scale = lax.rsqrt(fused[:, 3 * columns : 3 * columns + 1] / D + EPSILON)
    rows_new = (step_scale * fused[:, : 3 * columns] + qkv_bias.reshape(1, 3 * columns)).astype(
        jnp.bfloat16
    )
    rows_new = rows_new.reshape(STEPS, rollouts, 3 * columns)
    queries = rows_new[:, :, :columns]
    new_keys = rows_new[:, :, columns : 2 * columns]
    new_vals = rows_new[:, :, 2 * columns :]
    pooled_query = jnp.stack(
        [
            jnp.dot(onehot_half, queries[s], preferred_element_type=jnp.float32)
            for s in range(STEPS)
        ]
    )
    cache_all = jnp.sum(
        (pooled_query * cache_keys[None]).reshape(STEPS, half_rows, heads_here, piece_width),
        axis=-1,
    )
    new_all = jnp.sum(
        (
            queries.astype(jnp.float32)[:, None] * new_keys.astype(jnp.float32)[None]
        ).reshape(STEPS, STEPS, rollouts, heads_here, piece_width),
        axis=-1,
    )
    for bit_index in range(bit_count):
        swapped = partner((cache_all, new_all), "replica", bit_index)
        cache_all = cache_all + swapped[0]
        new_all = new_all + swapped[1]
    parts = []
    for turn_index in range(STEPS):
        cache_scores = jnp.where(filled, cache_all[turn_index] * inverse, NEGATIVE)
        new_scores = jnp.where(
            keep_new, new_all[turn_index, : turn_index + 1] * inverse, NEGATIVE
        )
        segment_top = jnp.max(
            jnp.where(onehot[:, :, None], cache_scores[:, None, :], NEGATIVE), axis=0
        )
        peak_val = jnp.maximum(segment_top, jnp.max(new_scores, axis=0))
        row_peak = jnp.dot(onehot_wide, peak_val, precision=lax.Precision.HIGHEST)
        cache_weights = jnp.exp(cache_scores - row_peak)
        new_weights = jnp.where(keep_new, jnp.exp(new_scores - peak_val[None]), 0.0)
        totals = jnp.dot(onehot_wide.T, cache_weights, precision=lax.Precision.HIGHEST) + jnp.sum(
            new_weights, axis=0
        )
        cache_rounded = spread_out(cache_weights.astype(jnp.bfloat16).astype(jnp.float32))
        accum = jnp.dot(onehot_wide.T, cache_rounded * cache_vals, precision=lax.Precision.HIGHEST)
        for item_index in range(turn_index + 1):
            new_rounded = spread_out(
                new_weights[item_index].astype(jnp.bfloat16).astype(jnp.float32)
            )
            accum = accum + new_rounded * new_vals[item_index].astype(jnp.float32)
        parts.append(jnp.concatenate([accum, totals, peak_val], axis=1))
    mine = jnp.stack(parts).reshape(new_count, columns + 2 * heads_here)
    both = lax.all_gather(mine, "tensor")

    def split(block):
        return block[:, columns + heads_here :], block[:, columns : columns + heads_here], block[:, :columns]

    _, total_all, accum_all = combine(split(both[0]), split(both[1]))
    attended = (accum_all / spread_out(total_all)).astype(jnp.bfloat16)
    attn_part = jnp.dot(attended, w_out, preferred_element_type=jnp.float32)
    middle = x_wide + lax.psum(attn_part, "replica")
    scaled_mid = (middle * norm_ffn).astype(jnp.bfloat16)
    gate_up = jnp.dot(
        scaled_mid, w_gateup.reshape(half_width, 2 * units), preferred_element_type=jnp.float32
    )
    mid_squares = jnp.sum(middle * middle, axis=1, keepdims=True)
    fused_mid = lax.psum(
        jnp.concatenate([gate_up, jnp.broadcast_to(mid_squares, (new_count, 128))], axis=1),
        "tensor",
    )
    mid_scale = lax.rsqrt(fused_mid[:, 2 * units : 2 * units + 1] / D + EPSILON)
    gate_vals = mid_scale * fused_mid[:, :units]
    up_vals = mid_scale * fused_mid[:, units : 2 * units]
    hidden_mid = (jax.nn.silu(gate_vals) * up_vals).astype(jnp.bfloat16)
    down_part = jnp.dot(hidden_mid, w_down, preferred_element_type=jnp.float32)
    result = middle + lax.psum(down_part, "replica")
    decoded = result.astype(jnp.bfloat16).reshape(STEPS, rollouts, half_width)
    return (decoded, kv_out)


def fused_kernel(
    hid_ref, len_ref, src_ref, page_ref, x_ref, gain_ref, gain2_ref, bias_ref,
    wq_hbm, wkv_hbm, wo_hbm, wgu_hbm, wd_hbm,
    dec_ref, pool_ref,
    area_a, area_b, area_c, hbuf, dacc, drecv, hacc, hsend, hrecv, sq, sqrecv,
    att, kvb, qb, nkv, psend, precv, zsend, zrecv, ag, guacc, gurecv, sq2, sq2recv, hm,
    wsem, hg_send, hg_fwd, hg_recv, ten_send, ten_recv,
    p_send, p_recv, z_send, z_recv, ag_send, ag_fwd, ag_recv,
):
    f32 = jnp.float32
    bf16 = jnp.bfloat16
    replicas = lax.axis_size("replica")
    depth = replicas // 2
    half = x_ref.shape[1]
    chunk = half // replicas
    cols = wq_hbm.shape[1]
    units = wd_hbm.shape[0]
    news = x_ref.shape[0]
    rolls = len_ref.shape[1]
    pad = hid_ref.shape[0]
    cached = replicas * pad
    me = lax.axis_index("replica")
    core = lax.axis_index("tensor")
    zed = me // 2
    ex = me % 2
    pair = {"replica": me + 1 - 2 * ex}
    other = {"tensor": 1 - core}
    mesh_id = pl.DeviceIdType.MESH

    def column(i):
        return 2 * ((zed + i) % depth) + ex

    wkv2 = wkv_hbm.reshape(2 * half, cols)
    wgu2 = wgu_hbm.reshape(2 * half, units)
    quarter = half // 2
    wq_copies = [
        pltpu.make_async_copy(
            wq_hbm.at[pl.ds(i * quarter, quarter)], area_b.at[pl.ds(i * quarter, quarter)], wsem.at[i]
        )
        for i in range(2)
    ]
    wkv_copies = [
        pltpu.make_async_copy(
            wkv2.at[pl.ds(i * quarter, quarter)], area_a.at[pl.ds(i * quarter, quarter)], wsem.at[2 + i]
        )
        for i in range(4)
    ]
    wgu_copy = pltpu.make_async_copy(wgu2, area_c, wsem.at[6])
    for copy in wq_copies + wkv_copies:
        copy.start()

    barrier = pltpu.get_barrier_semaphore()
    pl.semaphore_signal(barrier, inc=1, device_id=pair, device_id_type=mesh_id)
    pl.semaphore_signal(barrier, inc=1, device_id=other, device_id_type=mesh_id)
    for i in range(1, depth):
        pl.semaphore_signal(
            barrier, inc=1, device_id={"replica": column(i)}, device_id_type=mesh_id
        )
    hbuf[me] = hid_ref[...]
    pl.semaphore_wait(barrier, depth + 1)

    def remote(src, dst, send, recv, target):
        return pltpu.make_async_remote_copy(
            src_ref=src, dst_ref=dst, send_sem=send, recv_sem=recv,
            device_id=target, device_id_type=mesh_id,
        )

    def gather_start(buf, sends, recvs):
        for i in range(1, depth):
            remote(buf.at[me], buf.at[me], sends.at[i], recvs.at[me], {"replica": column(i)}).start()
        remote(buf.at[me], buf.at[me], sends.at[0], recvs.at[me], pair).start()

    def gather_step(n, buf, sends, fwds, recvs):
        turn = n % depth
        side = (ex + n // depth) % 2
        block = 2 * ((zed - turn + depth) % depth) + side
        arrived = remote(buf.at[block], buf.at[block], sends.at[0], recvs.at[block], pair)

        @pl.when(n > 0)
        def _():
            arrived.wait_recv()

        @pl.when((n > 0) & (n < depth))
        def _():
            remote(buf.at[block], buf.at[block], fwds.at[turn], recvs.at[block], pair).start()

        return block

    def gather_finish(buf, sends, fwds, recvs):
        for i in range(depth):
            remote(buf.at[me], buf.at[me], sends.at[i], recvs.at[me], pair).wait_send()
        for i in range(1, depth):
            remote(buf.at[me], buf.at[me], fwds.at[i], recvs.at[me], pair).wait_send()

    gather_start(hbuf, hg_send, hg_recv)
    wgu_copy.start()

    step = min(512, chunk)
    sq[pl.ds(0, news)] = jnp.zeros((news, 128), f32)

    @pl.loop(0, half // step)
    def _(k):
        at = pl.ds(pl.multiple_of(k * step, step), step)
        wide = x_ref[:, at].astype(f32)
        sq[pl.ds(0, news)] += jnp.broadcast_to(
            jnp.sum(wide * wide, axis=1, keepdims=True), (news, 128)
        )

    def scaled_new(at):
        return (x_ref[:, at].astype(f32) * gain_ref[:, at]).astype(bf16)

    spread_row = 2 * lax.broadcasted_iota(jnp.int32, (256, 512), 0)
    spread_col = lax.broadcasted_iota(jnp.int32, (256, 512), 1)
    even = (spread_col == spread_row).astype(bf16)
    odd = (spread_col == spread_row + 1).astype(bf16)

    def interleaved(piece):
        sides = []
        for each in (even, odd):
            outs = [
                jnp.dot(piece[:, j : j + 256], each, preferred_element_type=f32).astype(bf16)
                for j in range(0, piece.shape[1], 256)
            ]
            sides.append(jnp.concatenate(outs, axis=1))
        return jnp.concatenate(sides, axis=0)

    dacc[...] = jnp.zeros_like(dacc)
    for i in range(2):
        wq_copies[i].wait()

        @pl.loop(i * quarter // step, (i + 1) * quarter // step)
        def _(k):
            at = pl.ds(pl.multiple_of(k * step, step), step)
            dacc[pl.ds(0, news)] += jnp.dot(scaled_new(at), area_b[at], preferred_element_type=f32)

    wo_copies = [
        pltpu.make_async_copy(
            wo_hbm.at[:, pl.ds(i * cols, cols)], area_b.at[pl.ds(i * cols, cols)], wsem.at[7 + i]
        )
        for i in range(depth)
    ]
    for copy in wo_copies:
        copy.start()
    for i in range(4):
        wkv_copies[i].wait()

        @pl.loop(i * quarter // (2 * step), (i + 1) * quarter // (2 * step))
        def _(k):
            at = pl.ds(pl.multiple_of(k * step, step), step)
            at2 = pl.ds(pl.multiple_of(k * 2 * step, 2 * step), 2 * step)
            dacc[pl.ds(news, 2 * news)] += jnp.dot(
                interleaved(scaled_new(at)), area_a[at2], preferred_element_type=f32
            )

    swap_new = remote(dacc, drecv, ten_send.at[0], ten_recv.at[0], other)
    swap_new.start()

    @pl.loop(0, replicas)
    def _(n):
        block = gather_step(n, hbuf, hg_send, hg_fwd, hg_recv)
        rows = hbuf[block].astype(f32)
        sq[pl.ds(pl.multiple_of(news + block * pad, pad), pad)] = jnp.broadcast_to(
            jnp.sum(rows * rows, axis=1, keepdims=True), (pad, 128)
        )

    swap_sq = remote(sq, sqrecv, ten_send.at[1], ten_recv.at[1], other)
    swap_sq.start()
    hacc[...] = jnp.zeros_like(hacc)

    @pl.loop(0, half // step)
    def _(k):
        at = pl.ds(pl.multiple_of(k * step, step), step)
        at2 = pl.ds(pl.multiple_of(k * 2 * step, 2 * step), 2 * step)
        rows = hbuf[:, :, at].reshape(cached, step).astype(f32)
        scaled = (rows * gain_ref[:, at]).astype(bf16)
        hacc[...] += jnp.dot(interleaved(scaled), area_a[at2], preferred_element_type=f32)

    hsend[...] = hacc[...].astype(bf16)
    swap_kv = remote(hsend, hrecv, ten_send.at[2], ten_recv.at[2], other)
    swap_kv.start()
    wd_copies = [
        pltpu.make_async_copy(
            wd_hbm.at[:, pl.ds(i * cols, cols)], area_a.at[pl.ds(i * units, units)],
            wsem.at[7 + depth + i],
        )
        for i in range(depth)
    ]
    for copy in wd_copies:
        copy.start()

    square = (rolls, rolls)
    row_id = lax.broadcasted_iota(jnp.int32, square, 0)
    col_id = lax.broadcasted_iota(jnp.int32, square, 1)
    eye = row_id == col_id

    def upright(row):
        return jnp.sum(jnp.where(eye, row.astype(f32), 0.0), axis=1, keepdims=True)

    lengths = upright(len_ref[...])
    sources = upright(src_ref[...])
    earlier = (sources == src_ref[...].astype(f32)) & (col_id < row_id)
    offset = jnp.sum(jnp.where(earlier, len_ref[...].astype(f32), 0.0), axis=1, keepdims=True)
    slot = lax.broadcasted_iota(jnp.int32, (rolls, cached), 1)
    place = (slot % pad).astype(f32) - offset
    match = ((slot // pad).astype(f32) == sources) & (place >= 0.0) & (place < lengths)
    roll = lax.broadcasted_iota(jnp.int32, (rolls, cached), 0).astype(f32)
    owner = jnp.max(jnp.where(match, roll, -1.0), axis=0, keepdims=True)
    page = jnp.full((1, cached), -1.0, f32)
    for p in range(page_ref.shape[0]):
        picked = jnp.where(match & (place == p), upright(page_ref[pl.ds(p, 1)]), -1.0)
        page = jnp.maximum(page, jnp.max(picked, axis=0, keepdims=True))

    swap_new.wait()
    swap_sq.wait()
    totals = sq[...] + sqrecv[...]
    scale = lax.rsqrt(totals / D + EPSILON)[:, :1]
    new_scale = scale[:news]
    qb[...] = (
        new_scale * (dacc[pl.ds(0, news)] + drecv[pl.ds(0, news)]) + bias_ref[pl.ds(0, 1)]
    ).astype(bf16)
    for j in range(2):
        at = pl.ds((1 + j) * news, news)
        nkv[j] = (new_scale * (dacc[at] + drecv[at]) + bias_ref[pl.ds(1 + j, 1)]).astype(bf16)
    swap_kv.wait()
    for j in range(2):
        at = pl.ds(j * cached, cached)
        kvb[j] = (
            scale[news:] * (hacc[at] + hrecv[at].astype(f32)) + bias_ref[pl.ds(1 + j, 1)]
        ).astype(bf16)

    half_pool = pool_ref.shape[1]
    pick = (
        lax.broadcasted_iota(jnp.int32, (half_pool, cached), 0) + core * half_pool
    ).astype(f32) == page
    pick = pick.astype(bf16)
    for j in range(2):
        pool_ref[j] = jnp.dot(pick, kvb[j], preferred_element_type=f32).astype(bf16)

    token = lax.broadcasted_iota(jnp.int32, (news, cached), 0) % rolls
    old_ok = token.astype(f32) == owner
    t_row = lax.broadcasted_iota(jnp.int32, (news, news), 0)
    t_col = lax.broadcasted_iota(jnp.int32, (news, news), 1)
    new_ok = (t_row % rolls == t_col % rolls) & (t_col <= t_row)
    inverse = 1.0 / jnp.sqrt(jnp.float32(HD))
    across = (((1,), (1,)), ((), ()))
    for h in range(cols // HD):
        at = pl.ds(h * HD, HD)
        q = qb[:, at]
        old = lax.dot_general(q, kvb[0, :, at], across, preferred_element_type=f32)
        new = lax.dot_general(q, nkv[0, :, at], across, preferred_element_type=f32)
        old = jnp.where(old_ok, old * inverse, NEGATIVE)
        new = jnp.where(new_ok, new * inverse, NEGATIVE)
        peak = jnp.maximum(
            jnp.max(old, axis=1, keepdims=True), jnp.max(new, axis=1, keepdims=True)
        )
        old = jnp.exp(old - peak)
        new = jnp.exp(new - peak)
        total = jnp.sum(old, axis=1, keepdims=True) + jnp.sum(new, axis=1, keepdims=True)
        mixed = jnp.dot(old.astype(bf16), kvb[1, :, at], preferred_element_type=f32) + jnp.dot(
            new.astype(bf16), nkv[1, :, at], preferred_element_type=f32
        )
        att[:, at] = (mixed / total).astype(bf16)

    def reduce_chunks(which, lhs, area, depth_rows):
        def partial(zc, side):
            rows = pl.ds(pl.multiple_of(zc * depth_rows, depth_rows), depth_rows)
            lanes = pl.ds(pl.multiple_of(side * chunk, chunk), chunk)
            return jnp.dot(lhs[...], area[rows, lanes], preferred_element_type=f32)

        def to_pair(i):
            return remote(
                psend.at[i], precv.at[which, i], p_send.at[which, i], p_recv.at[which, i], pair
            )

        def to_column(i):
            return remote(
                zsend.at[i], zrecv.at[which, i], z_send.at[which, i], z_recv.at[which, i],
                {"replica": column(i)},
            )

        @pl.loop(1, depth + 1)
        def _(n):
            i = n % depth
            psend[i] = partial((zed + i) % depth, 1 - ex).astype(bf16)
            to_pair(i).start()

        @pl.loop(1, depth)
        def _(i):
            mine = partial((zed + i) % depth, ex)
            to_pair(i).wait_recv()
            zsend[i] = (mine + precv[which, i].astype(f32)).astype(bf16)
            to_column(i).start()

        result = partial(zed, ex)
        to_pair(0).wait_recv()
        result = result + precv[which, 0].astype(f32)
        for i in range(1, depth):
            to_column(i).wait_recv()
            result = result + zrecv[which, i].astype(f32)
        for i in range(depth):
            to_pair(i).wait_send()
            if i:
                to_column(i).wait_send()
        return result

    for copy in wo_copies:
        copy.wait()
    my_lanes = pl.ds(pl.multiple_of(me * chunk, chunk), chunk)
    ag[0, me] = reduce_chunks(0, att, area_b, cols).astype(bf16)
    first = (ag.at[0], ag_send.at[0], ag_fwd.at[0], ag_recv.at[0])
    gather_start(first[0], first[1], first[3])
    guacc[...] = jnp.zeros_like(guacc)
    sq2[...] = jnp.zeros_like(sq2)
    wgu_copy.wait()

    @pl.loop(0, replicas)
    def _(n):
        block = gather_step(n, *first)
        lanes = pl.ds(pl.multiple_of(block * chunk, chunk), chunk)
        middle = x_ref[:, lanes].astype(f32) + ag[0, block].astype(f32)
        sq2[...] += jnp.broadcast_to(jnp.sum(middle * middle, axis=1, keepdims=True), (news, 128))
        scaled = (middle * gain2_ref[:, lanes]).astype(bf16)
        rows = pl.ds(pl.multiple_of(block * 2 * chunk, 2 * chunk), 2 * chunk)
        guacc[...] += jnp.dot(interleaved(scaled), area_c[rows], preferred_element_type=f32)

    swap_gu = remote(guacc, gurecv, ten_send.at[3], ten_recv.at[3], other)
    swap_sq2 = remote(sq2, sq2recv, ten_send.at[4], ten_recv.at[4], other)
    swap_gu.start()
    swap_sq2.start()
    gather_finish(*first)
    for copy in wd_copies:
        copy.wait()
    swap_sq2.wait()
    mid_scale = lax.rsqrt((sq2[...] + sq2recv[...]) / D + EPSILON)[:, :1]
    swap_gu.wait()
    gate = mid_scale * (guacc[pl.ds(0, news)] + gurecv[pl.ds(0, news)])
    up = mid_scale * (guacc[pl.ds(news, news)] + gurecv[pl.ds(news, news)])
    hm[...] = (jax.nn.silu(gate) * up).astype(bf16)

    down = reduce_chunks(1, hm, area_a, units)
    middle = x_ref[:, my_lanes].astype(f32) + ag[0, me].astype(f32)
    ag[1, me] = (middle + down).astype(bf16)
    second = (ag.at[1], ag_send.at[1], ag_fwd.at[1], ag_recv.at[1])
    gather_start(second[0], second[1], second[3])

    @pl.loop(0, replicas)
    def _(n):
        block = gather_step(n, *second)
        dec_ref[:, pl.ds(pl.multiple_of(block * chunk, chunk), chunk)] = ag[1, block]

    gather_finish(*second)
    gather_finish(hbuf, hg_send, hg_fwd, hg_recv)


def fused_device(
    hidden, rollout_lengths, source_replica, page_table, x_new, norm_attn, norm_ffn,
    w_query, w_keyval, qkv_bias, w_out, w_gateup, w_down,
):
    replicas = lax.axis_size("replica")
    depth = replicas // 2
    slots, half = hidden.shape
    pad = -(-slots // 16) * 16
    cols = w_query.shape[1]
    units = w_down.shape[0]
    rolls, longest = page_table.shape
    news = STEPS * rolls
    cached = replicas * pad
    chunk = half // replicas
    f32, bf16 = jnp.float32, jnp.bfloat16
    vm = pltpu.VMEM
    dma = pltpu.SemaphoreType.DMA
    in_vmem = pl.BlockSpec(memory_space=pltpu.VMEM)
    in_hbm = pl.BlockSpec(memory_space=pl.ANY)
    decoded, pool = pl.pallas_call(
        fused_kernel,
        out_shape=(
            jax.ShapeDtypeStruct((news, half), bf16),
            jax.ShapeDtypeStruct((2, rolls * longest, cols), bf16),
        ),
        in_specs=[in_vmem] * 8 + [in_hbm] * 5,
        out_specs=(in_vmem, in_vmem),
        scratch_shapes=[
            vm((2 * half, cols), bf16),
            vm((half, cols), bf16),
            vm((2 * half, units), bf16),
            vm((replicas, pad, half), bf16),
            vm((3 * news, cols), f32),
            vm((3 * news, cols), f32),
            vm((2 * cached, cols), f32),
            vm((2 * cached, cols), bf16),
            vm((2 * cached, cols), bf16),
            vm((news + cached, 128), f32),
            vm((news + cached, 128), f32),
            vm((news, cols), bf16),
            vm((2, cached, cols), bf16),
            vm((news, cols), bf16),
            vm((2, news, cols), bf16),
            vm((depth, news, chunk), bf16),
            vm((2, depth, news, chunk), bf16),
            vm((depth, news, chunk), bf16),
            vm((2, depth, news, chunk), bf16),
            vm((2, replicas, news, chunk), bf16),
            vm((2 * news, units), f32),
            vm((2 * news, units), f32),
            vm((news, 128), f32),
            vm((news, 128), f32),
            vm((news, units), bf16),
            dma((7 + 2 * depth,)),
            dma((depth,)),
            dma((depth,)),
            dma((replicas,)),
            dma((5,)),
            dma((5,)),
            dma((2, depth)),
            dma((2, depth)),
            dma((2, depth)),
            dma((2, depth)),
            dma((2, depth)),
            dma((2, depth)),
            dma((2, replicas)),
        ],
        compiler_params=pltpu.CompilerParams(
            collective_id=0, has_side_effects=True, vmem_limit_bytes=VMEM_BYTES
        ),
        name="migrate_and_decode",
    )(
        jnp.pad(hidden, ((0, pad - slots), (0, 0))),
        rollout_lengths.reshape(1, rolls),
        source_replica.reshape(1, rolls),
        page_table.T,
        x_new.reshape(news, half),
        norm_attn.reshape(1, half),
        norm_ffn.reshape(1, half),
        qkv_bias,
        w_query,
        w_keyval,
        w_out,
        w_gateup,
        w_down,
    )
    return decoded.reshape(STEPS, rolls, half), pool


VMEM_BYTES = 63 * 2**20


def fits(mesh):
    replicas = mesh.shape["replica"]
    cols = D // replicas
    return replicas % 2 == 0 and replicas <= 8 and cols % (2 * HD) == 0 and cols <= 1024


def solution(mesh):
    placed = (
        P(("groups", "replica"), "tensor"),
        P("groups"),
        P("groups"),
        P("groups", None),
        P(None, "groups", "tensor"),
        P("tensor"),
        P("tensor"),
        P("tensor", "replica"),
        P("tensor", None, "replica"),
        P(None, "replica"),
        P("replica", "tensor"),
        P("tensor", None, "replica"),
        P("replica", "tensor"),
    )
    return jax.shard_map(
        fused_device if fits(mesh) else per_device,
        mesh=mesh,
        in_specs=placed,
        out_specs=(P(None, "groups", "tensor"), P(None, ("groups", "tensor"), "replica")),
        check_vma=False,
    )
```
